32 devices in a mesh: groups: 2 (over y), seq: 8 (over z, x), batch: 2 (over core).
Axes of the slice: x: 2, y: 2, z: 4, core: 2. Of those that a mesh axis runs over, the one named last changes fastest.
Arguments:
- tokens: int32 [4, 4096], P(('groups', 'batch'), 'seq'), parts along dimension 0, may hold values from 0 to 3
- hidden: bfloat16 [4, 4096, 1024], P(('groups', 'batch'), 'seq'), parts along dimension 0, may hold values from -6 to 6
- base_table: bfloat16 [4, 1024], replicated, may hold values from -6 to 6
- w_in: bfloat16 [1024, 2304], replicated, may hold values from -0.1875 to 0.1875
- w_dt: bfloat16 [1024, 16], replicated, may hold values from -0.1875 to 0.1875
- conv_w: float32 [4, 1280], replicated, may hold values from -3 to 3
- conv_b: float32 [1280], replicated, may hold values from -3 to 3
- dt_bias: float32 [16], replicated, as said below
- a_log: float32 [16], replicated, as said below
- d_skip: float32 [16], replicated, may hold values from 0.5 to 1.5
- norm_gain: float32 [1024], replicated, may hold values from 0.1 to 1.9
- w_out: bfloat16 [1024, 1024], replicated, may hold values from -0.1875 to 0.1875
Outputs:
- mixed: bfloat16 [4, 4096, 1024], P(('groups', 'batch'), 'seq'), parts along dimension 0
The draws below stay inside these ranges and needn't reach their ends.
There are 2 independent parts, one for each index of `groups`. The reference program is written for one: setup_inputs(seed, part) draws one part's arguments, and reference() takes and returns one part's arrays. A program takes and returns all parts, laid end to end along the dimension named above; an argument that names none is the same for every part. Nothing has to cross between parts.
Inputs may be any that keep to these rules, and one draw needn't show every extreme that they name: `a_log`: real numbers, one for each head. `dt_bias`: real numbers, one for each head.
All inputs are finite; a program needn't handle non-finite values.
Results may differ from the reference program's by a relative error of at most 0.0017.
The reference program's roundings to bfloat16 on the way count: a program that leaves them out, or rounds other values in their place, can miss the bound.
Values may be sent and summed in bfloat16 or wider, within the bound.
A program may use at most 192 MiB of HBM per device.

```python
import jax
import jax.numpy as jnp
from jax import lax

D = 1024
H = 16
P_SIZE = 64
N = 128
Q = 256
KCONV = 4
LENGTH = 4096
BATCH = 2


def head_kinds(key):
    picked = jax.random.uniform(jax.random.fold_in(key, 11), (H,))
    share = 0.5
    slow = picked < share
    jitter = jax.random.uniform(jax.random.fold_in(key, 12), (H,), minval=-0.7, maxval=0.7)
    return (slow, jitter)


def draw_a_log(key, part):
    slow, jitter = head_kinds(key)
    root = jnp.sqrt(jnp.float32(LENGTH))
    slow_rate = jnp.log(0.125 / root) + jitter
    fast_rate = jnp.log(0.07) + 0.5 * jitter
    return jnp.where(slow, slow_rate, fast_rate).astype(jnp.float32)


def draw_dt_bias(key, part):
    slow, jitter = head_kinds(key)
    root = jnp.sqrt(jnp.float32(LENGTH))
    slow_bias = jnp.log(jnp.expm1(4.0 / root * jnp.exp(0.4 * jitter)))
    fast_bias = 0.3 * jitter
    return jnp.where(slow, slow_bias, fast_bias).astype(jnp.float32)


def touch_ends(values, key, smallest, largest):
    dims = values.shape
    place = [jax.random.randint(jax.random.fold_in(key, axis), (), 0, dims[axis]) for axis in range(len(dims))]
    values = values.at[tuple(place)].set(smallest)
    longest = dims.index(max(dims))
    place[longest] = (place[longest] + 1) % dims[longest]
    return values.at[tuple(place)].set(largest)


def levels(own_key, extent, shards, least, high):
    def one(position, shards_of):
        steps = jax.random.uniform(jax.random.fold_in(jax.random.fold_in(own_key, 6), position), (shards_of,), jnp.float32, least / len(shards), high / len(shards))
        return jnp.repeat(jnp.exp(steps), extent[position] // shards_of).reshape((-1,) + (1,) * (len(extent) - position - 1))

    gain = one(*shards[0])
    for cut in shards[1:]:
        gain = gain * one(*cut)
    return gain


def gaussian(own_key, shape, deviation, most, split=(), kind=jnp.bfloat16):
    drawn = jax.random.normal(own_key, shape, jnp.float32) * deviation
    if len(split) > 0:
        drawn = levels(own_key, shape, split, -0.22, 0.18) * drawn
    return jnp.clip(drawn, min=-most, max=most).astype(kind)


def setup_inputs(seed: int = 0, part: int = 0) -> dict:
    streams_of = jax.random.split(jax.random.key(seed), 13)
    part_keys = jax.random.split(jax.random.fold_in(streams_of[12], part), 13)
    tokens = touch_ends(jax.random.randint(part_keys[0], (BATCH, LENGTH), 0, 4), jax.random.fold_in(part_keys[0], 1), 0, 3).astype(jnp.int32)
    hidden = gaussian(part_keys[1], (BATCH, LENGTH, D), 1.0, 6.0, ((0, 2), (1, 8)))
    base_table = gaussian(streams_of[2], (4, D), 1.0, 6.0)
    w_in = gaussian(streams_of[3], (D, 2 * H * P_SIZE + 2 * N), D ** -0.5, 0.1875)
    w_dt = gaussian(streams_of[4], (D, H), D ** -0.5, 0.1875)
    conv_w = gaussian(streams_of[5], (KCONV, H * P_SIZE + 2 * N), 0.5, 3.0, (), jnp.float32)
    conv_b = gaussian(streams_of[6], (H * P_SIZE + 2 * N,), 0.5, 3.0, (), jnp.float32)
    dt_bias = draw_dt_bias(jax.random.fold_in(streams_of[12], 71), part)
    a_log = draw_a_log(jax.random.fold_in(streams_of[12], 71), part)
    d_skip = jnp.clip(jax.random.uniform(streams_of[9], (H,), jnp.float32, 0.5, 1.5), 0.5, 1.5)
    norm_gain = jnp.clip(1.0 + 0.18 * jax.random.normal(streams_of[10], (H * P_SIZE,), jnp.float32), 0.1, 1.9)
    w_out = gaussian(streams_of[11], (H * P_SIZE, D), (H * P_SIZE) ** -0.5, 0.1875)
    return dict(tokens=tokens, hidden=hidden, base_table=base_table, w_in=w_in, w_dt=w_dt, conv_w=conv_w, conv_b=conv_b, dt_bias=dt_bias, a_log=a_log, d_skip=d_skip, norm_gain=norm_gain, w_out=w_out)


norm_epsilon = 1e-05

def span_terms(heads_x, b_rows, c_rows, step_size, rates):
    log_decay = jnp.cumsum(step_size * rates[None, :], axis=0)
    across = jnp.transpose(log_decay)
    width = across.shape[1]
    lower = (jnp.arange(width)[:, None] >= jnp.arange(width)[None, :])[None]
    gaps = across[:, :, None] - across[:, None, :]
    decays = jnp.where(lower, jnp.exp(jnp.where(lower, gaps, 0.0)), 0.0)
    scores = jnp.dot(c_rows, jnp.transpose(b_rows), preferred_element_type=jnp.float32)
    weights = (decays * scores[None] * jnp.transpose(step_size)[:, None, :]).astype(jnp.bfloat16)
    inside = jnp.einsum('hts,shp->thp', weights.astype(jnp.float32), heads_x.astype(jnp.float32))
    to_end = jnp.exp(log_decay[-1][None, :] - log_decay) * step_size
    state_weights = (b_rows.astype(jnp.float32)[:, None, :] * to_end[:, :, None]).astype(jnp.bfloat16)
    state = jnp.einsum('shp,shn->hpn', heads_x.astype(jnp.float32), state_weights.astype(jnp.float32))
    return (inside, state, jnp.exp(log_decay[-1]), jnp.exp(log_decay))

def mixer(strand, w_in, w_dt, conv_w, conv_b, dt_bias, a_log, d_skip, norm_gain, w_out):
    length = strand.shape[0]
    inner = H * P_SIZE
    projected = jnp.dot(strand, w_in, preferred_element_type=jnp.float32)
    gate_part = projected[:, :inner]
    source = projected[:, inner:]
    padded = jnp.concatenate([jnp.zeros((KCONV - 1, source.shape[1]), jnp.float32), source], axis=0)
    summed = jnp.broadcast_to(conv_b, source.shape)
    for tap in range(KCONV):
        summed = summed + conv_w[tap] * padded[tap:tap + length]
    activated = jax.nn.silu(summed).astype(jnp.bfloat16)
    step_size = jax.nn.softplus(jnp.dot(strand, w_dt, preferred_element_type=jnp.float32) + dt_bias)
    rates = -jnp.exp(a_log)
    spans = length // Q
    heads_x = activated[:, :inner].reshape(spans, Q, H, P_SIZE)
    b_rows = activated[:, inner:inner + N].reshape(spans, Q, N)
    c_rows = activated[:, inner + N:].reshape(spans, Q, N)
    steps_cut = step_size.reshape(spans, Q, H)

    def per_span(carry, pieces):
        piece_x, piece_b, piece_c, piece_s = pieces
        inside, state, total, from_start = span_terms(piece_x, piece_b, piece_c, piece_s, rates)
        carried = jnp.einsum('tn,hpn->thp', piece_c.astype(jnp.float32), carry, precision=lax.Precision.HIGHEST)
        result = inside + from_start[:, :, None] * carried + d_skip[None, :, None] * piece_x.astype(jnp.float32)
        return (total[:, None, None] * carry + state, result)
    start = jnp.zeros((H, P_SIZE, N), jnp.float32)
    final_state, results = lax.scan(per_span, start, (heads_x, b_rows, c_rows, steps_cut))
    scanned = results.reshape(length, inner)
    gated = scanned * jax.nn.silu(gate_part)
    normed = (gated * lax.rsqrt(lax.optimization_barrier(jnp.mean(gated * gated, axis=-1, keepdims=True)) + norm_epsilon) * norm_gain).astype(jnp.bfloat16)
    return jnp.dot(normed, w_out, preferred_element_type=jnp.float32)

def reference(tokens, hidden, base_table, w_in, w_dt, conv_w, conv_b, dt_bias, a_log, d_skip, norm_gain, w_out):
    results = []
    for slab in range(BATCH):
        looked = base_table[tokens[slab]].astype(jnp.float32)
        strand_input = (hidden[slab].astype(jnp.float32) + looked).astype(jnp.bfloat16)
        forward = mixer(strand_input, w_in, w_dt, conv_w, conv_b, dt_bias, a_log, d_skip, norm_gain, w_out)
        reverse = mixer(strand_input[::-1, ::-1], w_in, w_dt, conv_w, conv_b, dt_bias, a_log, d_skip, norm_gain, w_out)
        results.append((forward + reverse[::-1, ::-1]).astype(jnp.bfloat16))
    return jnp.stack(results)
```

```python
import functools

import jax
import jax.numpy as jnp
from jax import lax
from jax.experimental import pallas as pl
from jax.experimental.pallas import tpu as pltpu
from jax.sharding import PartitionSpec as P

H = 16
P_SIZE = 64
N = 128
Q = 256
KCONV = 4
D = 1024
INNER = H * P_SIZE
CONV = INNER + 2 * N
LANES = 128
CHUNKS = 2
HEADS_C = H // 2 // CHUNKS
ROWS_C = HEADS_C * P_SIZE
EDGE = 8

norm_epsilon = 1e-05
F32 = jnp.float32
BF16 = jnp.bfloat16
MESH = pl.DeviceIdType.MESH


def dot(a, b):
    return jnp.dot(a, b, preferred_element_type=F32)


def silu(a):
    half = 0.5 * a
    return half * (1.0 + jnp.tanh(half))


def kernel(
    rows, strand_ref, w_in_ref, w_dt_ref, conv_w_ref, conv_b_ref, dt_bias_ref, a_log_ref, d_skip_ref,
    gain_ref, w_out_ref, out_ref,
    v, source, halo, act, gate, inside, step, cum, cum_t, step_t, span_state, flipped_out,
    pack, pair_in, chain_in, chain_out, back_out, incoming,
    halo_send, halo_recv, pair_send, pair_recv, chain_send, chain_recv, back_send, back_recv,
):
    n = lax.axis_size("seq")
    me = lax.axis_index("seq")
    pairs = n // 2
    place, side = me // 2, me % 2
    other = 1 - side
    partner = me + 1 - 2 * side
    spans = rows // Q

    barrier = pltpu.get_barrier_semaphore()
    for off in (-2, -1, 1, 2):
        there = me + off

        @pl.when((there >= 0) & (there < n))
        def _(there=there):
            pl.semaphore_signal(barrier, inc=1, device_id={"seq": there}, device_id_type=MESH)

    pl.semaphore_wait(barrier, jnp.minimum(me, 2) + jnp.minimum(n - 1 - me, 2))

    row_id = lax.broadcasted_iota(jnp.int32, (Q, Q), 0)
    col_id = lax.broadcasted_iota(jnp.int32, (Q, Q), 1)
    exchange = jnp.where(row_id + col_id == Q - 1, 1.0, 0.0).astype(BF16)

    blocks = D // Q
    v[0] = strand_ref[...]
    for j in range(blocks):
        taken = strand_ref[:, (blocks - 1 - j) * Q : (blocks - j) * Q]
        v[1, :, j * Q : (j + 1) * Q] = dot(taken, exchange).astype(BF16)

    def halo_copy(strand):
        edge = rows if strand == 0 else EDGE
        return pltpu.make_async_remote_copy(
            src_ref=source.at[strand, pl.ds(edge, EDGE), :],
            dst_ref=halo.at[strand],
            send_sem=halo_send.at[strand],
            recv_sem=halo_recv.at[strand],
            device_id={"seq": me + 1 - 2 * strand},
            device_id_type=MESH,
        )

    def is_there(index):
        return (index >= 0) & (index < n)

    for strand in range(2):

        def columns_of(j, _, strand=strand):
            w_at = pl.ds(pl.multiple_of(INNER + j * Q, Q), Q)
            to = pl.ds(pl.multiple_of(j * Q, Q), Q)
            source[strand, EDGE : EDGE + rows, to] = dot(v[strand], w_in_ref[:, w_at])
            return 0

        lax.fori_loop(0, CONV // Q, columns_of, 0)

        @pl.when(is_there(me + 1 - 2 * strand))
        def _(strand=strand):
            halo_copy(strand).start()

    rates = -jnp.exp(a_log_ref[...])
    for strand in range(2):
        pre = dot(v[strand], w_dt_ref[...]) + dt_bias_ref[...]
        soft = jnp.maximum(pre, 0.0) + jnp.log1p(jnp.exp(-jnp.abs(pre)))
        step[strand] = soft
        keep = row_id >= col_id if strand == 0 else row_id <= col_id
        tri = jnp.where(keep, 1.0, 0.0).astype(F32)
        for span in range(spans):
            at = slice(span * Q, (span + 1) * Q)
            block_step = soft[at]
            total = jnp.dot(
                tri, block_step * rates, preferred_element_type=F32, precision=lax.Precision.HIGHEST
            )
            cum[strand, at, :] = total
            cum_t[strand, span] = jnp.transpose(total)[:H]
            step_t[strand, span] = jnp.transpose(block_step)[:H]

    for strand in range(2):
        first = 0 if strand == 0 else EDGE + rows

        @pl.when(is_there(me - 1 + 2 * strand))
        def _(strand=strand, first=first):
            halo_copy(strand).wait_recv()
            source[strand, first : first + EDGE, :] = halo[strand]

        @pl.when(jnp.logical_not(is_there(me - 1 + 2 * strand)))
        def _(strand=strand, first=first):
            source[strand, first : first + EDGE, :] = jnp.zeros((EDGE, CONV), F32)

        @pl.when(is_there(me + 1 - 2 * strand))
        def _(strand=strand):
            halo_copy(strand).wait_send()

        def conv_of(j, _, strand=strand):
            lanes = pl.ds(pl.multiple_of(j * LANES, LANES), LANES)
            for cut in range(0, rows, Q):
                summed = jnp.broadcast_to(conv_b_ref[:, lanes], (Q, LANES))
                for tap in range(KCONV):
                    shift = tap - KCONV + 1 if strand == 0 else KCONV - 1 - tap
                    low = EDGE + cut + shift
                    summed = summed + conv_w_ref[tap : tap + 1, lanes] * source[strand, low : low + Q, lanes]
                act[strand, cut : cut + Q, lanes] = silu(summed).astype(BF16)
            return 0

        lax.fori_loop(0, CONV // LANES, conv_of, 0)

        totals = []
        for span in range(spans):
            at = slice(span * Q, (span + 1) * Q)
            here = cum[strand, at, :]
            end = here[Q - 1 : Q] if strand == 0 else here[0:1]
            to_end = jnp.exp(end - here) * step[strand, at, :]
            b_rows = act[strand, at, INNER : INNER + N].astype(F32)
            for two in range(H // 2):
                x_two = act[strand, at, two * LANES : (two + 1) * LANES]
                both = jnp.concatenate(
                    [(b_rows * to_end[:, h : h + 1]).astype(BF16) for h in (2 * two, 2 * two + 1)], axis=1
                )
                prod = lax.dot_general(x_two, both, (((0,), (0,)), ((), ())), preferred_element_type=F32)
                low = two * LANES
                span_state[strand, span, low : low + P_SIZE] = prod[:P_SIZE, :N]
                span_state[strand, span, low + P_SIZE : low + LANES] = prod[P_SIZE:, N:]
            totals.append(jnp.exp(end))
        order = range(spans) if strand == 0 else range(spans - 1, -1, -1)
        for head in range(H):
            half, inner = divmod(head, H // 2)
            chunk, slot = divmod(inner, HEADS_C)
            at = slice(head * P_SIZE, (head + 1) * P_SIZE)
            state = None
            for span in order:
                one = totals[span][:, head : head + 1]
                if state is None:
                    state, decay = span_state[strand, span, at], one
                else:
                    state, decay = one * state + span_state[strand, span, at], one * decay
            pack[strand, half, chunk, slot * P_SIZE : (slot + 1) * P_SIZE] = state
            pack[strand, half, chunk, ROWS_C + slot : ROWS_C + slot + 1] = jnp.broadcast_to(decay, (1, N))
        for chunk in range(CHUNKS):
            for slot in range(HEADS_C, 8):
                for half in range(2):
                    pack[strand, half, chunk, ROWS_C + slot : ROWS_C + slot + 1] = jnp.zeros((1, N), F32)
            pair_copy = pltpu.make_async_remote_copy(
                src_ref=pack.at[strand, other, chunk],
                dst_ref=pair_in.at[strand, chunk],
                send_sem=pair_send.at[strand, chunk],
                recv_sem=pair_recv.at[strand, chunk],
                device_id={"seq": partner},
                device_id_type=MESH,
            )
            pair_copy.start()

    for strand in range(2):

        def gate_of(j, _, strand=strand):
            at = pl.ds(pl.multiple_of(j * Q, Q), Q)
            gate[strand, :, at] = silu(dot(v[strand], w_in_ref[:, at]))
            return 0

        lax.fori_loop(0, INNER // Q, gate_of, 0)
    for j in range(blocks):
        taken = w_out_ref[:, (blocks - 1 - j) * Q : (blocks - j) * Q]
        flipped_out[:, j * Q : (j + 1) * Q] = dot(taken, exchange).astype(BF16)

    def pair_of(strand, chunk):
        return pltpu.make_async_remote_copy(
            src_ref=pack.at[strand, other, chunk],
            dst_ref=pair_in.at[strand, chunk],
            send_sem=pair_send.at[strand, chunk],
            recv_sem=pair_recv.at[strand, chunk],
            device_id={"seq": partner},
            device_id_type=MESH,
        )

    def chain_of(strand, chunk):
        return pltpu.make_async_remote_copy(
            src_ref=chain_out.at[strand, chunk],
            dst_ref=chain_in.at[strand, chunk],
            send_sem=chain_send.at[strand, chunk],
            recv_sem=chain_recv.at[strand, chunk],
            device_id={"seq": me + 2 - 4 * strand},
            device_id_type=MESH,
        )

    def back_of(strand, chunk):
        return pltpu.make_async_remote_copy(
            src_ref=back_out.at[strand, chunk],
            dst_ref=incoming.at[strand, side, chunk],
            send_sem=back_send.at[strand, chunk],
            recv_sem=back_recv.at[strand, chunk],
            device_id={"seq": partner},
            device_id_type=MESH,
        )

    def hand_on(strand):
        earliest = (place + strand * (pairs - 1 - 2 * place)) == 0
        latest = (place + strand * (pairs - 1 - 2 * place)) == pairs - 1
        leads = side == strand
        for chunk in range(CHUNKS):
            pair_of(strand, chunk).wait_recv()

            @pl.when(earliest)
            def _(chunk=chunk):
                chain_in[strand, chunk] = jnp.zeros((ROWS_C, N), F32)

            @pl.when(jnp.logical_not(earliest))
            def _(chunk=chunk):
                chain_of(strand, chunk).wait_recv()

            for slot in range(HEADS_C):
                at = slice(slot * P_SIZE, (slot + 1) * P_SIZE)
                row = slice(ROWS_C + slot, ROWS_C + slot + 1)
                before = chain_in[strand, chunk, at]
                own = pack[strand, side, chunk, at]
                theirs = pair_in[strand, chunk, at]
                d_own = pack[strand, side, chunk, row]
                d_theirs = pair_in[strand, chunk, row]
                after_own = d_own * before + own
                after_theirs = d_theirs * before + theirs
                chain_out[strand, chunk, at] = jnp.where(
                    leads, d_theirs * after_own + theirs, d_own * after_theirs + own
                )
                back_out[strand, chunk, at] = jnp.where(leads, after_own, before)
                incoming[strand, side, chunk, at] = jnp.where(leads, before, after_theirs)

            @pl.when(jnp.logical_not(latest))
            def _(chunk=chunk):
                chain_of(strand, chunk).start()

            back_of(strand, chunk).start()

    half_q = Q // 2
    low_lanes = lax.broadcasted_iota(jnp.int32, (half_q, LANES), 1) < P_SIZE

    def inside_of(strand):
        def one_span(span, _):
            base = pl.multiple_of(span * Q, Q)
            b_rows = act[strand, pl.ds(base, Q), INNER : INNER + N]
            for part in range(2):
                top = pl.multiple_of(base + part * half_q, half_q)
                c_rows = act[strand, pl.ds(top, half_q), INNER + N :]
                whole = part == (1 if strand == 0 else 0)
                low, high = (0, Q) if whole else ((0, half_q) if strand == 0 else (half_q, Q))
                scores = lax.dot_general(
                    c_rows, b_rows[low:high], (((1,), (1,)), ((), ())), preferred_element_type=F32
                )
                t_id = lax.broadcasted_iota(jnp.int32, scores.shape, 0) + part * half_q
                s_id = lax.broadcasted_iota(jnp.int32, scores.shape, 1) + low
                scores = jnp.where(t_id >= s_id if strand == 0 else t_id <= s_id, scores, 0.0)
                here = cum[strand, pl.ds(top, half_q), :]
                for two in range(H // 2):
                    x_two = act[
                        strand, pl.ds(pl.multiple_of(base + low, half_q), high - low), two * LANES : (two + 1) * LANES
                    ]
                    found = []
                    for h in (2 * two, 2 * two + 1):
                        gaps = here[:, h : h + 1] - cum_t[strand, span, h : h + 1, low:high]
                        decays = jnp.exp(jnp.minimum(gaps, 0.0))
                        weights = (decays * scores * step_t[strand, span, h : h + 1, low:high]).astype(BF16)
                        found.append(dot(weights, x_two))
                    inside[strand, pl.ds(top, half_q), two * LANES : (two + 1) * LANES] = jnp.where(
                        low_lanes, found[0], found[1]
                    )
            return 0

        lax.fori_loop(0, spans, one_span, 0)

    lead = jnp.where(place < pairs // 2, 0, 1)
    hand_on(lead)
    inside_of(0)
    hand_on(1 - lead)
    inside_of(1)


    for strand in range(2):
        for chunk in range(CHUNKS):
            back_of(strand, chunk).wait_recv()

    low_lanes_q = lax.broadcasted_iota(jnp.int32, (Q, LANES), 1) < P_SIZE
    for strand in range(2):
        order = range(spans) if strand == 0 else range(spans - 1, -1, -1)
        previous = None
        for span in order:
            at = slice(span * Q, (span + 1) * Q)
            here = cum[strand, at, :]
            if previous is not None:
                last = previous * Q + (Q - 1 if strand == 0 else 0)
                total = jnp.exp(cum[strand, last : last + 1, :])
                for head in range(H):
                    half, inner = divmod(head, H // 2)
                    chunk, slot = divmod(inner, HEADS_C)
                    rows_h = slice(slot * P_SIZE, (slot + 1) * P_SIZE)
                    all_h = slice(head * P_SIZE, (head + 1) * P_SIZE)
                    incoming[strand, half, chunk, rows_h] = (
                        total[:, head : head + 1] * incoming[strand, half, chunk, rows_h]
                        + span_state[strand, previous, all_h]
                    )
            c_rows = act[strand, at, INNER + N :]
            c_both = jnp.concatenate([c_rows, c_rows], axis=1)
            grown = jnp.exp(here)
            squares = jnp.zeros((Q, 1), F32)
            for half in range(2):
                for chunk in range(CHUNKS):
                    start = incoming[strand, half, chunk]
                    upper = start.astype(BF16)
                    lower = (start - upper.astype(F32)).astype(BF16)
                    carried = lax.dot_general(
                        c_both,
                        jnp.concatenate([upper, lower], axis=1),
                        (((1,), (1,)), ((), ())),
                        preferred_element_type=F32,
                    )
                    head0 = half * (H // 2) + chunk * HEADS_C
                    for pos in range(HEADS_C // 2):
                        h = head0 + 2 * pos
                        lanes = slice(h * P_SIZE, h * P_SIZE + LANES)
                        scale = jnp.where(low_lanes_q, grown[:, h : h + 1], grown[:, h + 1 : h + 2])
                        scanned = (
                            inside[strand, at, lanes]
                            + scale * carried[:, pos * LANES : (pos + 1) * LANES]
                            + d_skip_ref[:, lanes] * act[strand, at, lanes].astype(F32)
                        )
                        gated = scanned * gate[strand, at, lanes]
                        inside[strand, at, lanes] = gated
                        squares = squares + jnp.sum(gated * gated, axis=1, keepdims=True)
            scale = lax.rsqrt(squares * (1.0 / INNER) + norm_epsilon)
            v[strand, at, :] = (inside[strand, at, :] * scale * gain_ref[...]).astype(BF16)
            previous = span

    def out_of(j, _):
        at = pl.ds(pl.multiple_of(j * Q, Q), Q)
        out_ref[:, at] = (dot(v[0], w_out_ref[:, at]) + dot(v[1], flipped_out[:, at])).astype(BF16)
        return 0

    lax.fori_loop(0, D // Q, out_of, 0)

    for strand in range(2):
        leaves = me + 2 - 4 * strand
        for chunk in range(CHUNKS):
            pair_of(strand, chunk).wait_send()
            back_of(strand, chunk).wait_send()

            @pl.when(is_there(leaves))
            def _(strand=strand, chunk=chunk):
                chain_of(strand, chunk).wait_send()


def on_device(
    tokens, hidden, base_table, w_in, w_dt, conv_w, conv_b, dt_bias, a_log, d_skip, norm_gain, w_out
):
    rows = hidden.shape[1]
    spans = rows // Q
    one_hot = (tokens[:, :, None] == jnp.arange(4)[None, None, :]).astype(BF16)
    looked = jnp.einsum("gtb,bd->gtd", one_hot, base_table, preferred_element_type=F32)
    strand_input = (hidden.astype(F32) + looked).astype(BF16)[0]
    wide = ((0, 0), (0, LANES - H))
    dma = pltpu.SemaphoreType.DMA
    outputs = pl.pallas_call(
        functools.partial(kernel, rows),
        out_shape=jax.ShapeDtypeStruct((rows, D), BF16),
        in_specs=[pl.BlockSpec(memory_space=pltpu.VMEM)] * 10,
        out_specs=pl.BlockSpec(memory_space=pltpu.VMEM),
        scratch_shapes=[
            pltpu.VMEM((2, rows, D), BF16),
            pltpu.VMEM((2, rows + 2 * EDGE, CONV), F32),
            pltpu.VMEM((2, EDGE, CONV), F32),
            pltpu.VMEM((2, rows, CONV), BF16),
            pltpu.VMEM((2, rows, INNER), F32),
            pltpu.VMEM((2, rows, INNER), F32),
            pltpu.VMEM((2, rows, LANES), F32),
            pltpu.VMEM((2, rows, LANES), F32),
            pltpu.VMEM((2, spans, H, Q), F32),
            pltpu.VMEM((2, spans, H, Q), F32),
            pltpu.VMEM((2, spans, INNER, N), F32),
            pltpu.VMEM((INNER, D), BF16),
            pltpu.VMEM((2, 2, CHUNKS, ROWS_C + 8, N), F32),
            pltpu.VMEM((2, CHUNKS, ROWS_C + 8, N), F32),
            pltpu.VMEM((2, CHUNKS, ROWS_C, N), F32),
            pltpu.VMEM((2, CHUNKS, ROWS_C, N), F32),
            pltpu.VMEM((2, CHUNKS, ROWS_C, N), F32),
            pltpu.VMEM((2, 2, CHUNKS, ROWS_C, N), F32),
            dma((2,)),
            dma((2,)),
            dma((2, CHUNKS)),
            dma((2, CHUNKS)),
            dma((2, CHUNKS)),
            dma((2, CHUNKS)),
            dma((2, CHUNKS)),
            dma((2, CHUNKS)),
        ],
        compiler_params=pltpu.CompilerParams(
            collective_id=0, has_side_effects=True, vmem_limit_bytes=58 * 1024 * 1024
        ),
    )(
        strand_input,
        w_in,
        jnp.pad(w_dt, wide),
        conv_w,
        conv_b[None],
        jnp.pad(dt_bias[None], wide),
        jnp.pad(a_log[None], wide),
        jnp.repeat(d_skip, P_SIZE)[None],
        norm_gain[None],
        w_out,
    )
    return outputs[None]


def solution(mesh):
    placed = (P(("groups", "batch"), "seq"), P(("groups", "batch"), "seq", None)) + (P(),) * 10
    return jax.shard_map(
        on_device,
        mesh=mesh,
        in_specs=placed,
        out_specs=P(("groups", "batch"), "seq", None),
        check_vma=False,
    )
```

```python
import functools

import jax
import jax.numpy as jnp
from jax import lax
from jax.experimental import pallas as pl
from jax.experimental.pallas import tpu as pltpu
from jax.sharding import PartitionSpec as P

H = 16
P_SIZE = 64
N = 128
Q = 256
KCONV = 4
D = 1024
INNER = H * P_SIZE
CONV = INNER + 2 * N
LANES = 128
CHUNKS = 2
HEADS_C = H // 2 // CHUNKS
ROWS_C = HEADS_C * P_SIZE
EDGE = 8

norm_epsilon = 1e-05
F32 = jnp.float32
BF16 = jnp.bfloat16
MESH = pl.DeviceIdType.MESH


def dot(a, b):
    return jnp.dot(a, b, preferred_element_type=F32)


def silu(a):
    half = 0.5 * a
    return half * (1.0 + jnp.tanh(half))


def kernel(
    rows, tokens_ref, hidden_ref, table_ref, w_in_ref, w_dt_ref, conv_w_ref, conv_b_ref, dt_bias_ref, a_log_ref, d_skip_ref,
    gain_ref, w_out_ref, out_ref,
    table, wide_dt, small, d_wide, v, source, halo, act, gate, inside, step, cum, cum_t, step_t, span_state, flipped_out,
    pack, pair_in, chain_in, chain_out, back_out, incoming,
    halo_send, halo_recv, pair_send, pair_recv, chain_send, chain_recv, back_send, back_recv,
):
    n = lax.axis_size("seq")
    me = lax.axis_index("seq")
    pairs = n // 2
    place, side = me // 2, me % 2
    other = 1 - side
    partner = me + 1 - 2 * side
    spans = rows // Q

    barrier = pltpu.get_barrier_semaphore()
    for off in (-2, -1, 1, 2):
        there = me + off

        @pl.when((there >= 0) & (there < n))
        def _(there=there):
            pl.semaphore_signal(barrier, inc=1, device_id={"seq": there}, device_id_type=MESH)

    pl.semaphore_wait(barrier, jnp.minimum(me, 2) + jnp.minimum(n - 1 - me, 2))

    row_id = lax.broadcasted_iota(jnp.int32, (Q, Q), 0)
    col_id = lax.broadcasted_iota(jnp.int32, (Q, Q), 1)
    exchange = jnp.where(row_id + col_id == Q - 1, 1.0, 0.0).astype(BF16)

    blocks = D // Q
    table[...] = jnp.zeros((EDGE, D), F32)
    table[:4] = table_ref[...].astype(F32)
    lookup = jnp.concatenate([table[...], jnp.zeros((EDGE, D), F32)], axis=0).astype(BF16)
    base_id = lax.broadcasted_iota(jnp.int32, (2 * EDGE, rows), 0)
    one_hot = jnp.where(base_id == tokens_ref[...], 1.0, 0.0).astype(BF16)
    for j in range(blocks):
        at = slice(j * Q, (j + 1) * Q)
        looked = lax.dot_general(one_hot, lookup[:, at], (((0,), (0,)), ((), ())), preferred_element_type=F32)
        v[0, :, at] = (hidden_ref[0, :, at].astype(F32) + looked).astype(BF16)
    for j in range(blocks):
        taken = v[0, :, (blocks - 1 - j) * Q : (blocks - j) * Q]
        v[1, :, j * Q : (j + 1) * Q] = dot(taken, exchange).astype(BF16)

    def halo_copy(strand):
        edge = rows if strand == 0 else EDGE
        return pltpu.make_async_remote_copy(
            src_ref=source.at[strand, pl.ds(edge, EDGE), :],
            dst_ref=halo.at[strand],
            send_sem=halo_send.at[strand],
            recv_sem=halo_recv.at[strand],
            device_id={"seq": me + 1 - 2 * strand},
            device_id_type=MESH,
        )

    def is_there(index):
        return (index >= 0) & (index < n)

    for strand in range(2):

        def columns_of(j, _, strand=strand):
            w_at = pl.ds(pl.multiple_of(INNER + j * Q, Q), Q)
            to = pl.ds(pl.multiple_of(j * Q, Q), Q)
            source[strand, EDGE : EDGE + rows, to] = dot(v[strand], w_in_ref[:, w_at])
            return 0

        lax.fori_loop(0, CONV // Q, columns_of, 0)

        @pl.when(is_there(me + 1 - 2 * strand))
        def _(strand=strand):
            halo_copy(strand).start()

    wide_dt[...] = jnp.zeros((LANES, D), BF16)
    wide_dt[:H] = w_dt_ref[...]
    small[...] = jnp.zeros((EDGE, LANES), F32)
    small[0:1, :H] = dt_bias_ref[...]
    small[1:2, :H] = a_log_ref[...]
    low_lanes_one = lax.broadcasted_iota(jnp.int32, (1, LANES), 1) < P_SIZE
    skips = d_skip_ref[...]
    for two in range(H // 2):
        d_wide[:, two * LANES : (two + 1) * LANES] = jnp.where(
            low_lanes_one, skips[:, 2 * two : 2 * two + 1], skips[:, 2 * two + 1 : 2 * two + 2]
        )
    rates = -jnp.exp(small[1:2])
    for strand in range(2):
        pre = lax.dot_general(
            v[strand], wide_dt[...], (((1,), (1,)), ((), ())), preferred_element_type=F32
        ) + small[0:1]
        soft = jnp.maximum(pre, 0.0) + jnp.log1p(jnp.exp(-jnp.abs(pre)))
        step[strand] = soft
        keep = row_id >= col_id if strand == 0 else row_id <= col_id
        tri = jnp.where(keep, 1.0, 0.0).astype(F32)
        for span in range(spans):
            at = slice(span * Q, (span + 1) * Q)
            block_step = soft[at]
            total = jnp.dot(
                tri, block_step * rates, preferred_element_type=F32, precision=lax.Precision.HIGHEST
            )
            cum[strand, at, :] = total
            cum_t[strand, span] = jnp.transpose(total)[:H]
            step_t[strand, span] = jnp.transpose(block_step)[:H]

    for strand in range(2):
        first = 0 if strand == 0 else EDGE + rows

        @pl.when(is_there(me - 1 + 2 * strand))
        def _(strand=strand, first=first):
            halo_copy(strand).wait_recv()
            source[strand, first : first + EDGE, :] = halo[strand]

        @pl.when(jnp.logical_not(is_there(me - 1 + 2 * strand)))
        def _(strand=strand, first=first):
            source[strand, first : first + EDGE, :] = jnp.zeros((EDGE, CONV), F32)

        @pl.when(is_there(me + 1 - 2 * strand))
        def _(strand=strand):
            halo_copy(strand).wait_send()

        def conv_of(j, _, strand=strand):
            lanes = pl.ds(pl.multiple_of(j * LANES, LANES), LANES)
            for cut in range(0, rows, Q):
                summed = jnp.broadcast_to(conv_b_ref[pl.ds(j, 1), :], (Q, LANES))
                for tap in range(KCONV):
                    shift = tap - KCONV + 1 if strand == 0 else KCONV - 1 - tap
                    low = EDGE + cut + shift
                    summed = summed + conv_w_ref[tap : tap + 1, lanes] * source[strand, low : low + Q, lanes]
                act[strand, cut : cut + Q, lanes] = silu(summed).astype(BF16)
            return 0

        lax.fori_loop(0, CONV // LANES, conv_of, 0)

        totals = []
        for span in range(spans):
            at = slice(span * Q, (span + 1) * Q)
            here = cum[strand, at, :]
            end = here[Q - 1 : Q] if strand == 0 else here[0:1]
            to_end = jnp.exp(end - here) * step[strand, at, :]
            b_rows = act[strand, at, INNER : INNER + N].astype(F32)
            for two in range(H // 2):
                x_two = act[strand, at, two * LANES : (two + 1) * LANES]
                both = jnp.concatenate(
                    [(b_rows * to_end[:, h : h + 1]).astype(BF16) for h in (2 * two, 2 * two + 1)], axis=1
                )
                prod = lax.dot_general(x_two, both, (((0,), (0,)), ((), ())), preferred_element_type=F32)
                low = two * LANES
                span_state[strand, span, low : low + P_SIZE] = prod[:P_SIZE, :N]
                span_state[strand, span, low + P_SIZE : low + LANES] = prod[P_SIZE:, N:]
            totals.append(jnp.exp(end))
        order = range(spans) if strand == 0 else range(spans - 1, -1, -1)
        for head in range(H):
            half, inner = divmod(head, H // 2)
            chunk, slot = divmod(inner, HEADS_C)
            at = slice(head * P_SIZE, (head + 1) * P_SIZE)
            state = None
            for span in order:
                one = totals[span][:, head : head + 1]
                if state is None:
                    state, decay = span_state[strand, span, at], one
                else:
                    state, decay = one * state + span_state[strand, span, at], one * decay
            pack[strand, half, chunk, slot * P_SIZE : (slot + 1) * P_SIZE] = state
            pack[strand, half, chunk, ROWS_C + slot : ROWS_C + slot + 1] = jnp.broadcast_to(decay, (1, N))
        for chunk in range(CHUNKS):
            for slot in range(HEADS_C, 8):
                for half in range(2):
                    pack[strand, half, chunk, ROWS_C + slot : ROWS_C + slot + 1] = jnp.zeros((1, N), F32)
            pair_copy = pltpu.make_async_remote_copy(
                src_ref=pack.at[strand, other, chunk],
                dst_ref=pair_in.at[strand, chunk],
                send_sem=pair_send.at[strand, chunk],
                recv_sem=pair_recv.at[strand, chunk],
                device_id={"seq": partner},
                device_id_type=MESH,
            )
            pair_copy.start()

    for strand in range(2):

        def gate_of(j, _, strand=strand):
            at = pl.ds(pl.multiple_of(j * Q, Q), Q)
            gate[strand, :, at] = silu(dot(v[strand], w_in_ref[:, at]))
            return 0

        lax.fori_loop(0, INNER // Q, gate_of, 0)
    for j in range(blocks):
        taken = w_out_ref[:, (blocks - 1 - j) * Q : (blocks - j) * Q]
        flipped_out[:, j * Q : (j + 1) * Q] = dot(taken, exchange).astype(BF16)

    def pair_of(strand, chunk):
        return pltpu.make_async_remote_copy(
            src_ref=pack.at[strand, other, chunk],
            dst_ref=pair_in.at[strand, chunk],
            send_sem=pair_send.at[strand, chunk],
            recv_sem=pair_recv.at[strand, chunk],
            device_id={"seq": partner},
            device_id_type=MESH,
        )

    def chain_of(strand, chunk):
        return pltpu.make_async_remote_copy(
            src_ref=chain_out.at[strand, chunk],
            dst_ref=chain_in.at[strand, chunk],
            send_sem=chain_send.at[strand, chunk],
            recv_sem=chain_recv.at[strand, chunk],
            device_id={"seq": me + 2 - 4 * strand},
            device_id_type=MESH,
        )

    def back_of(strand, chunk):
        return pltpu.make_async_remote_copy(
            src_ref=back_out.at[strand, chunk],
            dst_ref=incoming.at[strand, side, chunk],
            send_sem=back_send.at[strand, chunk],
            recv_sem=back_recv.at[strand, chunk],
            device_id={"seq": partner},
            device_id_type=MESH,
        )

    def hand_on(strand):
        earliest = (place + strand * (pairs - 1 - 2 * place)) == 0
        latest = (place + strand * (pairs - 1 - 2 * place)) == pairs - 1
        leads = side == strand
        for chunk in range(CHUNKS):
            pair_of(strand, chunk).wait_recv()

            @pl.when(earliest)
            def _(chunk=chunk):
                chain_in[strand, chunk] = jnp.zeros((ROWS_C, N), F32)

            @pl.when(jnp.logical_not(earliest))
            def _(chunk=chunk):
                chain_of(strand, chunk).wait_recv()

            for slot in range(HEADS_C):
                at = slice(slot * P_SIZE, (slot + 1) * P_SIZE)
                row = slice(ROWS_C + slot, ROWS_C + slot + 1)
                before = chain_in[strand, chunk, at]
                own = pack[strand, side, chunk, at]
                theirs = pair_in[strand, chunk, at]
                d_own = pack[strand, side, chunk, row]
                d_theirs = pair_in[strand, chunk, row]
                after_own = d_own * before + own
                after_theirs = d_theirs * before + theirs
                chain_out[strand, chunk, at] = jnp.where(
                    leads, d_theirs * after_own + theirs, d_own * after_theirs + own
                )
                back_out[strand, chunk, at] = jnp.where(leads, after_own, before)
                incoming[strand, side, chunk, at] = jnp.where(leads, before, after_theirs)

            @pl.when(jnp.logical_not(latest))
            def _(chunk=chunk):
                chain_of(strand, chunk).start()

            back_of(strand, chunk).start()

    half_q = Q // 2
    low_lanes = lax.broadcasted_iota(jnp.int32, (half_q, LANES), 1) < P_SIZE

    def inside_of(strand):
        def one_span(span, _):
            base = pl.multiple_of(span * Q, Q)
            b_rows = act[strand, pl.ds(base, Q), INNER : INNER + N]
            for part in range(2):
                top = pl.multiple_of(base + part * half_q, half_q)
                c_rows = act[strand, pl.ds(top, half_q), INNER + N :]
                whole = part == (1 if strand == 0 else 0)
                low, high = (0, Q) if whole else ((0, half_q) if strand == 0 else (half_q, Q))
                scores = lax.dot_general(
                    c_rows, b_rows[low:high], (((1,), (1,)), ((), ())), preferred_element_type=F32
                )
                t_id = lax.broadcasted_iota(jnp.int32, scores.shape, 0) + part * half_q
                s_id = lax.broadcasted_iota(jnp.int32, scores.shape, 1) + low
                scores = jnp.where(t_id >= s_id if strand == 0 else t_id <= s_id, scores, 0.0)
                here = cum[strand, pl.ds(top, half_q), :]
                for two in range(H // 2):
                    x_two = act[
                        strand, pl.ds(pl.multiple_of(base + low, half_q), high - low), two * LANES : (two + 1) * LANES
                    ]
                    found = []
                    for h in (2 * two, 2 * two + 1):
                        gaps = here[:, h : h + 1] - cum_t[strand, span, h : h + 1, low:high]
                        decays = jnp.exp(jnp.minimum(gaps, 0.0))
                        weights = (decays * scores * step_t[strand, span, h : h + 1, low:high]).astype(BF16)
                        found.append(dot(weights, x_two))
                    inside[strand, pl.ds(top, half_q), two * LANES : (two + 1) * LANES] = jnp.where(
                        low_lanes, found[0], found[1]
                    )
            return 0

        lax.fori_loop(0, spans, one_span, 0)

    lead = jnp.where(place < pairs // 2, 0, 1)
    hand_on(lead)
    inside_of(0)
    hand_on(1 - lead)
    inside_of(1)


    for strand in range(2):
        for chunk in range(CHUNKS):
            back_of(strand, chunk).wait_recv()

    low_lanes_q = lax.broadcasted_iota(jnp.int32, (Q, LANES), 1) < P_SIZE
    for strand in range(2):
        order = range(spans) if strand == 0 else range(spans - 1, -1, -1)
        previous = None
        for span in order:
            at = slice(span * Q, (span + 1) * Q)
            here = cum[strand, at, :]
            if previous is not None:
                last = previous * Q + (Q - 1 if strand == 0 else 0)
                total = jnp.exp(cum[strand, last : last + 1, :])
                for head in range(H):
                    half, inner = divmod(head, H // 2)
                    chunk, slot = divmod(inner, HEADS_C)
                    rows_h = slice(slot * P_SIZE, (slot + 1) * P_SIZE)
                    all_h = slice(head * P_SIZE, (head + 1) * P_SIZE)
                    incoming[strand, half, chunk, rows_h] = (
                        total[:, head : head + 1] * incoming[strand, half, chunk, rows_h]
                        + span_state[strand, previous, all_h]
                    )
            c_rows = act[strand, at, INNER + N :]
            c_both = jnp.concatenate([c_rows, c_rows], axis=1)
            grown = jnp.exp(here)
            squares = jnp.zeros((Q, 1), F32)
            for half in range(2):
                for chunk in range(CHUNKS):
                    start = incoming[strand, half, chunk]
                    upper = start.astype(BF16)
                    lower = (start - upper.astype(F32)).astype(BF16)
                    carried = lax.dot_general(
                        c_both,
                        jnp.concatenate([upper, lower], axis=1),
                        (((1,), (1,)), ((), ())),
                        preferred_element_type=F32,
                    )
                    head0 = half * (H // 2) + chunk * HEADS_C
                    for pos in range(HEADS_C // 2):
                        h = head0 + 2 * pos
                        lanes = slice(h * P_SIZE, h * P_SIZE + LANES)
                        scale = jnp.where(low_lanes_q, grown[:, h : h + 1], grown[:, h + 1 : h + 2])
                        scanned = (
                            inside[strand, at, lanes]
                            + scale * carried[:, pos * LANES : (pos + 1) * LANES]
                            + d_wide[:, lanes] * act[strand, at, lanes].astype(F32)
                        )
                        gated = scanned * gate[strand, at, lanes]
                        inside[strand, at, lanes] = gated
                        squares = squares + jnp.sum(gated * gated, axis=1, keepdims=True)
            scale = lax.rsqrt(squares * (1.0 / INNER) + norm_epsilon)
            v[strand, at, :] = (inside[strand, at, :] * scale * gain_ref[...]).astype(BF16)
            previous = span

    def out_of(j, _):
        at = pl.ds(pl.multiple_of(j * Q, Q), Q)
        out_ref[:, at] = (dot(v[0], w_out_ref[:, at]) + dot(v[1], flipped_out[:, at])).astype(BF16)
        return 0

    lax.fori_loop(0, D // Q, out_of, 0)

    for strand in range(2):
        leaves = me + 2 - 4 * strand
        for chunk in range(CHUNKS):
            pair_of(strand, chunk).wait_send()
            back_of(strand, chunk).wait_send()

            @pl.when(is_there(leaves))
            def _(strand=strand, chunk=chunk):
                chain_of(strand, chunk).wait_send()


def on_device(
    tokens, hidden, base_table, w_in, w_dt, conv_w, conv_b, dt_bias, a_log, d_skip, norm_gain, w_out
):
    rows = hidden.shape[1]
    spans = rows // Q
    dma = pltpu.SemaphoreType.DMA
    outputs = pl.pallas_call(
        functools.partial(kernel, rows),
        out_shape=jax.ShapeDtypeStruct((rows, D), BF16),
        in_specs=[pl.BlockSpec(memory_space=pltpu.VMEM)] * 12,
        out_specs=pl.BlockSpec(memory_space=pltpu.VMEM),
        scratch_shapes=[
            pltpu.VMEM((EDGE, D), F32),
            pltpu.VMEM((LANES, D), BF16),
            pltpu.VMEM((EDGE, LANES), F32),
            pltpu.VMEM((1, INNER), F32),
            pltpu.VMEM((2, rows, D), BF16),
            pltpu.VMEM((2, rows + 2 * EDGE, CONV), F32),
            pltpu.VMEM((2, EDGE, CONV), F32),
            pltpu.VMEM((2, rows, CONV), BF16),
            pltpu.VMEM((2, rows, INNER), F32),
            pltpu.VMEM((2, rows, INNER), F32),
            pltpu.VMEM((2, rows, LANES), F32),
            pltpu.VMEM((2, rows, LANES), F32),
            pltpu.VMEM((2, spans, H, Q), F32),
            pltpu.VMEM((2, spans, H, Q), F32),
            pltpu.VMEM((2, spans, INNER, N), F32),
            pltpu.VMEM((INNER, D), BF16),
            pltpu.VMEM((2, 2, CHUNKS, ROWS_C + 8, N), F32),
            pltpu.VMEM((2, CHUNKS, ROWS_C + 8, N), F32),
            pltpu.VMEM((2, CHUNKS, ROWS_C, N), F32),
            pltpu.VMEM((2, CHUNKS, ROWS_C, N), F32),
            pltpu.VMEM((2, CHUNKS, ROWS_C, N), F32),
            pltpu.VMEM((2, 2, CHUNKS, ROWS_C, N), F32),
            dma((2,)),
            dma((2,)),
            dma((2, CHUNKS)),
            dma((2, CHUNKS)),
            dma((2, CHUNKS)),
            dma((2, CHUNKS)),
            dma((2, CHUNKS)),
            dma((2, CHUNKS)),
        ],
        compiler_params=pltpu.CompilerParams(
            collective_id=0, has_side_effects=True, vmem_limit_bytes=58 * 1024 * 1024
        ),
    )(
        tokens,
        hidden,
        base_table,
        w_in,
        w_dt.T,
        conv_w,
        conv_b.reshape(CONV // LANES, LANES),
        dt_bias[None],
        a_log[None],
        d_skip[None],
        norm_gain[None],
        w_out,
    )
    return outputs[None]


def solution(mesh):
    placed = (P(("groups", "batch"), "seq"), P(("groups", "batch"), "seq", None)) + (P(),) * 10
    return jax.shard_map(
        on_device,
        mesh=mesh,
        in_specs=placed,
        out_specs=P(("groups", "batch"), "seq", None),
        check_vma=False,
    )
```

```python
import functools

import jax
import jax.numpy as jnp
from jax import lax
from jax.experimental import pallas as pl
from jax.experimental.pallas import tpu as pltpu
from jax.sharding import PartitionSpec as P

H = 16
P_SIZE = 64
N = 128
Q = 256
KCONV = 4
D = 1024
INNER = H * P_SIZE
CONV = INNER + 2 * N
LANES = 128
CHUNKS = 4
HEADS_C = H // 2 // CHUNKS
ROWS_C = HEADS_C * P_SIZE
EDGE = 8

norm_epsilon = 1e-05
F32 = jnp.float32
BF16 = jnp.bfloat16
MESH = pl.DeviceIdType.MESH


def dot(a, b):
    return jnp.dot(a, b, preferred_element_type=F32)


def silu(a):
    half = 0.5 * a
    return half * (1.0 + jnp.tanh(half))


def kernel(
    rows, tokens_ref, hidden_ref, table_ref, w_in_ref, w_dt_ref, conv_w_ref, conv_b_ref, dt_bias_ref, a_log_ref, d_skip_ref,
    gain_ref, w_out_ref, out_ref,
    table, wide_dt, small, d_wide, v, source, halo, act, gate, inside, step, cum, cum_t, step_t, span_state, flipped_out,
    pack, pair_in, chain_in, chain_out, back_out, incoming,
    halo_send, halo_recv, pair_send, pair_recv, chain_send, chain_recv, back_send, back_recv,
):
    n = lax.axis_size("seq")
    me = lax.axis_index("seq")
    pairs = n // 2
    place, side = me // 2, me % 2
    other = 1 - side
    partner = me + 1 - 2 * side
    spans = rows // Q

    barrier = pltpu.get_barrier_semaphore()
    for off in (-2, -1, 1, 2):
        there = me + off

        @pl.when((there >= 0) & (there < n))
        def _(there=there):
            pl.semaphore_signal(barrier, inc=1, device_id={"seq": there}, device_id_type=MESH)

    pl.semaphore_wait(barrier, jnp.minimum(me, 2) + jnp.minimum(n - 1 - me, 2))

    row_id = lax.broadcasted_iota(jnp.int32, (Q, Q), 0)
    col_id = lax.broadcasted_iota(jnp.int32, (Q, Q), 1)
    exchange = jnp.where(row_id + col_id == Q - 1, 1.0, 0.0).astype(BF16)

    blocks = D // Q
    table[...] = jnp.zeros((EDGE, D), F32)
    table[:4] = table_ref[...].astype(F32)
    lookup = jnp.concatenate([table[...], jnp.zeros((EDGE, D), F32)], axis=0).astype(BF16)
    base_id = lax.broadcasted_iota(jnp.int32, (2 * EDGE, rows), 0)
    one_hot = jnp.where(base_id == tokens_ref[...], 1.0, 0.0).astype(BF16)
    for j in range(blocks):
        at = slice(j * Q, (j + 1) * Q)
        looked = lax.dot_general(one_hot, lookup[:, at], (((0,), (0,)), ((), ())), preferred_element_type=F32)
        v[0, :, at] = (hidden_ref[0, :, at].astype(F32) + looked).astype(BF16)
    for j in range(blocks):
        taken = v[0, :, (blocks - 1 - j) * Q : (blocks - j) * Q]
        v[1, :, j * Q : (j + 1) * Q] = dot(taken, exchange).astype(BF16)

    def halo_copy(strand):
        edge = rows if strand == 0 else EDGE
        return pltpu.make_async_remote_copy(
            src_ref=source.at[strand, pl.ds(edge, EDGE), :],
            dst_ref=halo.at[strand],
            send_sem=halo_send.at[strand],
            recv_sem=halo_recv.at[strand],
            device_id={"seq": me + 1 - 2 * strand},
            device_id_type=MESH,
        )

    def is_there(index):
        return (index >= 0) & (index < n)

    for strand in range(2):

        def columns_of(j, _, strand=strand):
            w_at = pl.ds(pl.multiple_of(INNER + j * Q, Q), Q)
            to = pl.ds(pl.multiple_of(j * Q, Q), Q)
            source[strand, EDGE : EDGE + rows, to] = dot(v[strand], w_in_ref[:, w_at])
            return 0

        lax.fori_loop(0, CONV // Q, columns_of, 0)

        @pl.when(is_there(me + 1 - 2 * strand))
        def _(strand=strand):
            halo_copy(strand).start()

    wide_dt[...] = jnp.zeros((LANES, D), BF16)
    wide_dt[:H] = w_dt_ref[...]
    small[...] = jnp.zeros((EDGE, LANES), F32)
    small[0:1, :H] = dt_bias_ref[...]
    small[1:2, :H] = a_log_ref[...]
    low_lanes_one = lax.broadcasted_iota(jnp.int32, (1, LANES), 1) < P_SIZE
    skips = d_skip_ref[...]
    for two in range(H // 2):
        d_wide[:, two * LANES : (two + 1) * LANES] = jnp.where(
            low_lanes_one, skips[:, 2 * two : 2 * two + 1], skips[:, 2 * two + 1 : 2 * two + 2]
        )
    rates = -jnp.exp(small[1:2])
    for strand in range(2):
        pre = lax.dot_general(
            v[strand], wide_dt[...], (((1,), (1,)), ((), ())), preferred_element_type=F32
        ) + small[0:1]
        soft = jnp.maximum(pre, 0.0) + jnp.log1p(jnp.exp(-jnp.abs(pre)))
        step[strand] = soft
        keep = row_id >= col_id if strand == 0 else row_id <= col_id
        tri = jnp.where(keep, 1.0, 0.0).astype(F32)
        for span in range(spans):
            at = slice(span * Q, (span + 1) * Q)
            block_step = soft[at]
            total = jnp.dot(
                tri, block_step * rates, preferred_element_type=F32, precision=lax.Precision.HIGHEST
            )
            cum[strand, at, :] = total
            cum_t[strand, span] = jnp.transpose(total)[:H]
            step_t[strand, span] = jnp.transpose(block_step)[:H]

    for strand in range(2):
        first = 0 if strand == 0 else EDGE + rows

        @pl.when(is_there(me - 1 + 2 * strand))
        def _(strand=strand, first=first):
            halo_copy(strand).wait_recv()
            source[strand, first : first + EDGE, :] = halo[strand]

        @pl.when(jnp.logical_not(is_there(me - 1 + 2 * strand)))
        def _(strand=strand, first=first):
            source[strand, first : first + EDGE, :] = jnp.zeros((EDGE, CONV), F32)

        @pl.when(is_there(me + 1 - 2 * strand))
        def _(strand=strand):
            halo_copy(strand).wait_send()

        def conv_of(j, _, strand=strand):
            lanes = pl.ds(pl.multiple_of(j * LANES, LANES), LANES)
            for cut in range(0, rows, Q):
                summed = jnp.broadcast_to(conv_b_ref[pl.ds(j, 1), :], (Q, LANES))
                for tap in range(KCONV):
                    shift = tap - KCONV + 1 if strand == 0 else KCONV - 1 - tap
                    low = EDGE + cut + shift
                    summed = summed + conv_w_ref[tap : tap + 1, lanes] * source[strand, low : low + Q, lanes]
                act[strand, cut : cut + Q, lanes] = silu(summed).astype(BF16)
            return 0

        lax.fori_loop(0, CONV // LANES, conv_of, 0)

        totals = []
        for span in range(spans):
            at = slice(span * Q, (span + 1) * Q)
            here = cum[strand, at, :]
            end = here[Q - 1 : Q] if strand == 0 else here[0:1]
            to_end = jnp.exp(end - here) * step[strand, at, :]
            b_rows = act[strand, at, INNER : INNER + N].astype(F32)
            for two in range(H // 2):
                x_two = act[strand, at, two * LANES : (two + 1) * LANES]
                both = jnp.concatenate(
                    [(b_rows * to_end[:, h : h + 1]).astype(BF16) for h in (2 * two, 2 * two + 1)], axis=1
                )
                prod = lax.dot_general(x_two, both, (((0,), (0,)), ((), ())), preferred_element_type=F32)
                low = two * LANES
                span_state[strand, span, low : low + P_SIZE] = prod[:P_SIZE, :N]
                span_state[strand, span, low + P_SIZE : low + LANES] = prod[P_SIZE:, N:]
            totals.append(jnp.exp(end))
        order = range(spans) if strand == 0 else range(spans - 1, -1, -1)
        for head in range(H):
            half, inner = divmod(head, H // 2)
            chunk, slot = divmod(inner, HEADS_C)
            at = slice(head * P_SIZE, (head + 1) * P_SIZE)
            state = None
            for span in order:
                one = totals[span][:, head : head + 1]
                if state is None:
                    state, decay = span_state[strand, span, at], one
                else:
                    state, decay = one * state + span_state[strand, span, at], one * decay
            pack[strand, half, chunk, slot * P_SIZE : (slot + 1) * P_SIZE] = state
            pack[strand, half, chunk, ROWS_C + slot : ROWS_C + slot + 1] = jnp.broadcast_to(decay, (1, N))
        for chunk in range(CHUNKS):
            for slot in range(HEADS_C, 8):
                for half in range(2):
                    pack[strand, half, chunk, ROWS_C + slot : ROWS_C + slot + 1] = jnp.zeros((1, N), F32)
            pair_copy = pltpu.make_async_remote_copy(
                src_ref=pack.at[strand, other, chunk],
                dst_ref=pair_in.at[strand, chunk],
                send_sem=pair_send.at[strand, chunk],
                recv_sem=pair_recv.at[strand, chunk],
                device_id={"seq": partner},
                device_id_type=MESH,
            )
            pair_copy.start()

    for strand in range(2):

        def gate_of(j, _, strand=strand):
            at = pl.ds(pl.multiple_of(j * Q, Q), Q)
            gate[strand, :, at] = silu(dot(v[strand], w_in_ref[:, at]))
            return 0

        lax.fori_loop(0, INNER // Q, gate_of, 0)
    for j in range(blocks):
        taken = w_out_ref[:, (blocks - 1 - j) * Q : (blocks - j) * Q]
        flipped_out[:, j * Q : (j + 1) * Q] = dot(taken, exchange).astype(BF16)

    def pair_of(strand, chunk):
        return pltpu.make_async_remote_copy(
            src_ref=pack.at[strand, other, chunk],
            dst_ref=pair_in.at[strand, chunk],
            send_sem=pair_send.at[strand, chunk],
            recv_sem=pair_recv.at[strand, chunk],
            device_id={"seq": partner},
            device_id_type=MESH,
        )

    def chain_of(strand, chunk):
        return pltpu.make_async_remote_copy(
            src_ref=chain_out.at[strand, chunk],
            dst_ref=chain_in.at[strand, chunk],
            send_sem=chain_send.at[strand, chunk],
            recv_sem=chain_recv.at[strand, chunk],
            device_id={"seq": me + 2 - 4 * strand},
            device_id_type=MESH,
        )

    def back_of(strand, chunk):
        return pltpu.make_async_remote_copy(
            src_ref=back_out.at[strand, chunk],
            dst_ref=incoming.at[strand, side, chunk],
            send_sem=back_send.at[strand, chunk],
            recv_sem=back_recv.at[strand, chunk],
            device_id={"seq": partner},
            device_id_type=MESH,
        )

    def hand_on(strand):
        earliest = (place + strand * (pairs - 1 - 2 * place)) == 0
        latest = (place + strand * (pairs - 1 - 2 * place)) == pairs - 1
        leads = side == strand
        for chunk in range(CHUNKS):
            pair_of(strand, chunk).wait_recv()

            @pl.when(earliest)
            def _(chunk=chunk):
                chain_in[strand, chunk] = jnp.zeros((ROWS_C, N), F32)

            @pl.when(jnp.logical_not(earliest))
            def _(chunk=chunk):
                chain_of(strand, chunk).wait_recv()

            for slot in range(HEADS_C):
                at = slice(slot * P_SIZE, (slot + 1) * P_SIZE)
                row = slice(ROWS_C + slot, ROWS_C + slot + 1)
                before = chain_in[strand, chunk, at]
                own = pack[strand, side, chunk, at]
                theirs = pair_in[strand, chunk, at]
                d_own = pack[strand, side, chunk, row]
                d_theirs = pair_in[strand, chunk, row]
                after_own = d_own * before + own
                after_theirs = d_theirs * before + theirs
                chain_out[strand, chunk, at] = jnp.where(
                    leads, d_theirs * after_own + theirs, d_own * after_theirs + own
                )
                back_out[strand, chunk, at] = jnp.where(leads, after_own, before)
                incoming[strand, side, chunk, at] = jnp.where(leads, before, after_theirs)

            @pl.when(jnp.logical_not(latest))
            def _(chunk=chunk):
                chain_of(strand, chunk).start()

            back_of(strand, chunk).start()

    half_q = Q // 2
    low_lanes = lax.broadcasted_iota(jnp.int32, (half_q, LANES), 1) < P_SIZE

    def inside_of(strand):
        def one_span(span, _):
            base = pl.multiple_of(span * Q, Q)
            b_rows = act[strand, pl.ds(base, Q), INNER : INNER + N]
            for part in range(2):
                top = pl.multiple_of(base + part * half_q, half_q)
                c_rows = act[strand, pl.ds(top, half_q), INNER + N :]
                whole = part == (1 if strand == 0 else 0)
                low, high = (0, Q) if whole else ((0, half_q) if strand == 0 else (half_q, Q))
                scores = lax.dot_general(
                    c_rows, b_rows[low:high], (((1,), (1,)), ((), ())), preferred_element_type=F32
                )
                t_id = lax.broadcasted_iota(jnp.int32, scores.shape, 0) + part * half_q
                s_id = lax.broadcasted_iota(jnp.int32, scores.shape, 1) + low
                scores = jnp.where(t_id >= s_id if strand == 0 else t_id <= s_id, scores, 0.0)
                here = cum[strand, pl.ds(top, half_q), :]
                for two in range(H // 2):
                    x_two = act[
                        strand, pl.ds(pl.multiple_of(base + low, half_q), high - low), two * LANES : (two + 1) * LANES
                    ]
                    found = []
                    for h in (2 * two, 2 * two + 1):
                        gaps = here[:, h : h + 1] - cum_t[strand, span, h : h + 1, low:high]
                        decays = jnp.exp(jnp.minimum(gaps, 0.0))
                        weights = (decays * scores * step_t[strand, span, h : h + 1, low:high]).astype(BF16)
                        found.append(dot(weights, x_two))
                    inside[strand, pl.ds(top, half_q), two * LANES : (two + 1) * LANES] = jnp.where(
                        low_lanes, found[0], found[1]
                    )
            return 0

        lax.fori_loop(0, spans, one_span, 0)

    lead = jnp.where(place < pairs // 2, 0, 1)
    hand_on(lead)
    inside_of(0)
    hand_on(1 - lead)
    inside_of(1)


    for strand in range(2):
        for chunk in range(CHUNKS):
            back_of(strand, chunk).wait_recv()

    low_lanes_q = lax.broadcasted_iota(jnp.int32, (Q, LANES), 1) < P_SIZE
    for strand in range(2):
        order = range(spans) if strand == 0 else range(spans - 1, -1, -1)
        previous = None
        for span in order:
            at = slice(span * Q, (span + 1) * Q)
            here = cum[strand, at, :]
            if previous is not None:
                last = previous * Q + (Q - 1 if strand == 0 else 0)
                total = jnp.exp(cum[strand, last : last + 1, :])
                for head in range(H):
                    half, inner = divmod(head, H // 2)
                    chunk, slot = divmod(inner, HEADS_C)
                    rows_h = slice(slot * P_SIZE, (slot + 1) * P_SIZE)
                    all_h = slice(head * P_SIZE, (head + 1) * P_SIZE)
                    incoming[strand, half, chunk, rows_h] = (
                        total[:, head : head + 1] * incoming[strand, half, chunk, rows_h]
                        + span_state[strand, previous, all_h]
                    )
            c_rows = act[strand, at, INNER + N :]
            c_both = jnp.concatenate([c_rows, c_rows], axis=1)
            grown = jnp.exp(here)
            squares = jnp.zeros((Q, 1), F32)
            for half in range(2):
                for chunk in range(CHUNKS):
                    start = incoming[strand, half, chunk]
                    upper = start.astype(BF16)
                    lower = (start - upper.astype(F32)).astype(BF16)
                    carried = lax.dot_general(
                        c_both,
                        jnp.concatenate([upper, lower], axis=1),
                        (((1,), (1,)), ((), ())),
                        preferred_element_type=F32,
                    )
                    head0 = half * (H // 2) + chunk * HEADS_C
                    for pos in range(HEADS_C // 2):
                        h = head0 + 2 * pos
                        lanes = slice(h * P_SIZE, h * P_SIZE + LANES)
                        scale = jnp.where(low_lanes_q, grown[:, h : h + 1], grown[:, h + 1 : h + 2])
                        scanned = (
                            inside[strand, at, lanes]
                            + scale * carried[:, pos * LANES : (pos + 1) * LANES]
                            + d_wide[:, lanes] * act[strand, at, lanes].astype(F32)
                        )
                        gated = scanned * gate[strand, at, lanes]
                        inside[strand, at, lanes] = gated
                        squares = squares + jnp.sum(gated * gated, axis=1, keepdims=True)
            scale = lax.rsqrt(squares * (1.0 / INNER) + norm_epsilon)
            v[strand, at, :] = (inside[strand, at, :] * scale * gain_ref[...]).astype(BF16)
            previous = span

    def out_of(j, _):
        at = pl.ds(pl.multiple_of(j * Q, Q), Q)
        out_ref[:, at] = (dot(v[0], w_out_ref[:, at]) + dot(v[1], flipped_out[:, at])).astype(BF16)
        return 0

    lax.fori_loop(0, D // Q, out_of, 0)

    for strand in range(2):
        leaves = me + 2 - 4 * strand
        for chunk in range(CHUNKS):
            pair_of(strand, chunk).wait_send()
            back_of(strand, chunk).wait_send()

            @pl.when(is_there(leaves))
            def _(strand=strand, chunk=chunk):
                chain_of(strand, chunk).wait_send()


def on_device(
    tokens, hidden, base_table, w_in, w_dt, conv_w, conv_b, dt_bias, a_log, d_skip, norm_gain, w_out
):
    rows = hidden.shape[1]
    spans = rows // Q
    dma = pltpu.SemaphoreType.DMA
    outputs = pl.pallas_call(
        functools.partial(kernel, rows),
        out_shape=jax.ShapeDtypeStruct((rows, D), BF16),
        in_specs=[pl.BlockSpec(memory_space=pltpu.VMEM)] * 12,
        out_specs=pl.BlockSpec(memory_space=pltpu.VMEM),
        scratch_shapes=[
            pltpu.VMEM((EDGE, D), F32),
            pltpu.VMEM((LANES, D), BF16),
            pltpu.VMEM((EDGE, LANES), F32),
            pltpu.VMEM((1, INNER), F32),
            pltpu.VMEM((2, rows, D), BF16),
            pltpu.VMEM((2, rows + 2 * EDGE, CONV), F32),
            pltpu.VMEM((2, EDGE, CONV), F32),
            pltpu.VMEM((2, rows, CONV), BF16),
            pltpu.VMEM((2, rows, INNER), F32),
            pltpu.VMEM((2, rows, INNER), F32),
            pltpu.VMEM((2, rows, LANES), F32),
            pltpu.VMEM((2, rows, LANES), F32),
            pltpu.VMEM((2, spans, H, Q), F32),
            pltpu.VMEM((2, spans, H, Q), F32),
            pltpu.VMEM((2, spans, INNER, N), F32),
            pltpu.VMEM((INNER, D), BF16),
            pltpu.VMEM((2, 2, CHUNKS, ROWS_C + 8, N), F32),
            pltpu.VMEM((2, CHUNKS, ROWS_C + 8, N), F32),
            pltpu.VMEM((2, CHUNKS, ROWS_C, N), F32),
            pltpu.VMEM((2, CHUNKS, ROWS_C, N), F32),
            pltpu.VMEM((2, CHUNKS, ROWS_C, N), F32),
            pltpu.VMEM((2, 2, CHUNKS, ROWS_C, N), F32),
            dma((2,)),
            dma((2,)),
            dma((2, CHUNKS)),
            dma((2, CHUNKS)),
            dma((2, CHUNKS)),
            dma((2, CHUNKS)),
            dma((2, CHUNKS)),
            dma((2, CHUNKS)),
        ],
        compiler_params=pltpu.CompilerParams(
            collective_id=0, has_side_effects=True, vmem_limit_bytes=58 * 1024 * 1024
        ),
    )(
        tokens,
        hidden,
        base_table,
        w_in,
        w_dt.T,
        conv_w,
        conv_b.reshape(CONV // LANES, LANES),
        dt_bias[None],
        a_log[None],
        d_skip[None],
        norm_gain[None],
        w_out,
    )
    return outputs[None]


def solution(mesh):
    placed = (P(("groups", "batch"), "seq"), P(("groups", "batch"), "seq", None)) + (P(),) * 10
    return jax.shard_map(
        on_device,
        mesh=mesh,
        in_specs=placed,
        out_specs=P(("groups", "batch"), "seq", None),
        check_vma=False,
    )
```
